32 devices in a mesh: groups: 2 (over x), dev: 16 (over z, y, core).
Axes of the slice: x: 2, y: 2, z: 4, core: 2. Of those that a mesh axis runs over, the one named last changes fastest.
Arguments:
- request_query_rows: bfloat16 [96, 6144], P(('groups', 'dev')), parts along dimension 0, may hold values from -6 to 6
- new_kv: bfloat16 [96, 2048], P(('groups', 'dev')), parts along dimension 0, may hold values from -6 to 6
- kv_pool: bfloat16 [448, 16, 2048], P(('groups', 'dev')), parts along dimension 0, may hold values from -6 to 6
- page_table: int32 [32, 14], P(('groups', 'dev')), parts along dimension 0, may hold values from 0 to 13, each once within a row
- page_count: int32 [32, 3], P(('groups', 'dev')), parts along dimension 0, may hold values from 1 to 8, 14 in all within a row
- last_fill: int32 [32, 3], P(('groups', 'dev')), parts along dimension 0, may hold values from 1 to 16
- mig_slot: int32 [32, 3], P(('groups', 'dev')), parts along dimension 0, may hold values from 0 to 2, as said below
- residual: bfloat16 [96, 6144], P(('groups', 'dev')), parts along dimension 0, may hold values from -36 to 36
- norm_gain: float32 [6144], replicated, may hold values from 0.1 to 1.9
- route_ids: int32 [96, 2], P(('groups', 'dev')), parts along dimension 0, may hold values from 0 to 7, all different within a row; in each aligned block of 3 rows (0 to 2, 3 to 5, ...) at most 3 rows name the same one
- route_logit: bfloat16 [96, 2], P(('groups', 'dev')), parts along dimension 0, may hold values from -6 to 6
- w_gate: bfloat16 [6144, 2048], P(None, 'dev'), may hold values from -0.078125 to 0.078125
- w_up: bfloat16 [6144, 2048], P(None, 'dev'), may hold values from -0.078125 to 0.078125
- w_down: bfloat16 [2048, 6144], P('dev'), may hold values from -0.1875 to 0.1875
Outputs:
- layer_out: bfloat16 [96, 6144], P(('groups', 'dev')), parts along dimension 0
- arrived_cache: bfloat16 [96, 128, 2048], P(('groups', 'dev')), parts along dimension 0
The draws below stay inside these ranges and needn't reach their ends.
There are 2 independent parts, one for each index of `groups`. The reference program is written for one: setup_inputs(seed, part) draws one part's arguments, and reference() takes and returns one part's arrays. A program takes and returns all parts, laid end to end along the dimension named above; an argument that names none is the same for every part. Nothing has to cross between parts.
Inputs may be any that keep to these rules, and one draw needn't show every extreme that they name: `mig_slot`: the entries of one instance's row differ. `route_ids`: each row names 2 different experts; among the 3 rows of one instance, before migration, no expert is named by more than 3 rows.
All inputs are finite; a program needn't handle non-finite values.
Results may differ from the reference program's by a relative error of at most 0.0028.
Values may be sent and summed in bfloat16 or wider, within the bound.
A program may use at most 64 MiB of HBM per device.

```python
import math
import jax
import jax.numpy as jnp
import numpy as np
from jax import lax

D = 6144
QUERY_HEADS = 48
KEY_VALUE_HEADS = 8
HEAD_SIZE = 128
EXPERTS = 8
TOPK = 2
REQ_DEV = 3
MOST = 3
PAGE = 16
MAXP = 8
NBITS = 3
POOL = 14
CACHE_LENGTH = 128
TOK = 48
QW = 6144
KVW = 2048
FFW = 2048
N_DEV = 16


def draw_request_query_rows(key, part):
    key = jax.random.fold_in(key, 11)
    values = jnp.clip(jax.random.normal(key, (TOK, QW), jnp.float32), -6.0, 6.0)
    return values.astype(jnp.bfloat16)


def draw_new_kv(key, part):
    key = jax.random.fold_in(key, 21)
    values = jnp.clip(jax.random.normal(key, (TOK, KVW), jnp.float32), -6.0, 6.0)
    return values.astype(jnp.bfloat16)


def draw_kv_pool(key, part):
    key = jax.random.fold_in(key, 31)
    values = jnp.clip(jax.random.normal(key, (N_DEV * POOL, PAGE, KVW), jnp.float32), -6.0, 6.0)
    return values.astype(jnp.bfloat16)


def draw_residual(key, part):
    key = jax.random.fold_in(key, 41)
    row_key, col_key, value_key = jax.random.split(key, 3)
    row_scale = jnp.exp(jax.random.uniform(row_key, (TOK, 1), jnp.float32, math.log(0.3), math.log(3.0)))
    col_scale = jnp.exp(jax.random.uniform(col_key, (1, D), jnp.float32, math.log(0.3), math.log(3.0)))
    values = jnp.clip(jax.random.normal(value_key, (TOK, D), jnp.float32), -4.0, 4.0)
    return (values * row_scale * col_scale).astype(jnp.bfloat16)


def draw_mig_slot(key, part):
    key = jax.random.fold_in(key, 51)
    device_keys = jax.random.split(key, N_DEV)

    def one_row(device_key):
        return jax.random.permutation(device_key, REQ_DEV)[:NBITS]
    return jax.vmap(one_row)(device_keys).astype(jnp.int32)


def with_ends(result, stream_key, smallest, top_value):
    place = [jax.random.randint(jax.random.fold_in(stream_key, axis), (), 0, length) for axis, length in enumerate(result.shape)]
    longest = result.shape.index(max(result.shape))
    beside = place[:longest] + [(place[longest] + 1) % result.shape[longest]] + place[longest + 1:]
    return result.at[tuple(place)].set(smallest).at[tuple(beside)].set(top_value)


def raised(drawn, rng, source, target, blocks, factor):
    owner, partner = [(jnp.arange(drawn.shape[dim]) // (drawn.shape[dim] // blocks)).reshape([-1 if axis == dim else 1 for axis in range(drawn.ndim)]) for dim in (source, target)]
    chosen = jax.random.permutation(rng, blocks)[partner]
    strong = (owner == chosen) | (owner == (partner + blocks // 2) % blocks)
    return jnp.where(strong, factor * drawn, drawn)


def shard_levels(stream_key, shape, cuts, smallest, largest):
    def one(position, shards_of):
        heights = jax.random.uniform(jax.random.fold_in(jax.random.fold_in(stream_key, 6), position), (shards_of,), jnp.float32, smallest / len(cuts), largest / len(cuts))
        return jnp.repeat(jnp.exp(heights), shape[position] // shards_of).reshape((-1,) + (1,) * (len(shape) - position - 1))

    gain = one(*cuts[0])
    for cut in cuts[1:]:
        gain = gain * one(*cut)
    return gain


def split_up(number_of, total, reach, slope):
    weights = [(1 << 20) // math.isqrt(grade ** slope) + 1 for grade in range(2, number_of + 1)]
    rest, given = total - reach - (number_of - 1), [1] * (number_of - 1)
    while rest > 0:
        candidates = [i for i in range(number_of - 1) if given[i] < reach]
        mass, left = sum([weights[i] for i in candidates]), rest
        for i in candidates:
            more = min(reach - given[i], max(1, left * weights[i] // mass), rest)
            given[i] = given[i] + more
            rest = rest - more
    return np.array([reach] + given)


def uneven(rng, amount, total, bound, lean):
    if amount == 2:
        one = jax.random.randint(rng, (), max(1, total - bound), min(bound, total - 1) + 1)
        return jnp.stack([one, total - one])
    sizes = jnp.asarray(split_up(amount, total, bound, lean), jnp.int32)
    couples = (amount - 1) // 2
    giver, taker = sizes[1:1 + 2 * couples:2], sizes[2:2 + 2 * couples:2]
    margin = jnp.minimum(giver - 1, bound - taker)
    passed = jax.random.randint(jax.random.fold_in(rng, 1), (couples,), 0, 1 << 20) % (margin + 1)
    sizes = sizes.at[1:1 + 2 * couples:2].set(giver - passed).at[2:2 + 2 * couples:2].set(taker + passed)
    return sizes[jax.random.permutation(jax.random.fold_in(rng, 2), amount)]


def shared_out(stream_key, own, number, rows, amount, top, limit, lean):
    ranking = jax.random.permutation(stream_key, amount)
    crowded, common = load_shares(amount, rows * top, limit, lean, True), load_shares(amount, rows * top, limit, lean, False)
    places = jnp.arange(amount)

    def named(sizes, offset_by):
        used = int((sizes > 0).sum())
        fixed = max(1, used // 4)
        shifted = fixed + (places - fixed + offset_by * (used - fixed)) % max(1, amount - fixed)
        return jnp.zeros((amount,), jnp.int32).at[ranking[jnp.where(places < fixed, places, shifted)]].set(jnp.asarray(sizes, jnp.int32))

    sizes = jnp.where(number % 4 == 0, named(crowded, number // 4), named(common, number - number // 4 - 1))
    mixed = jax.random.permutation(jax.random.fold_in(own, 3), amount)
    giver, receiver = mixed[0:amount // 2 * 2:2], mixed[1:amount // 2 * 2:2]
    margin = jnp.minimum(sizes[giver] - 1, limit - sizes[receiver]) // 2
    margin = jnp.where((giver == ranking[0]) | (receiver == ranking[0]) | (sizes[receiver] == 0), 0, jnp.maximum(margin, 0))
    shifted = jax.random.randint(jax.random.fold_in(own, 4), (amount // 2,), 0, 1 << 20) % (margin + 1)
    sizes = sizes.at[giver].add(-shifted).at[receiver].add(shifted)
    members = jnp.searchsorted(jnp.cumsum(sizes), jnp.arange(rows * top), side="right").astype(jnp.int32)
    table = members.reshape(top, rows).T
    table = table[jax.random.permutation(jax.random.fold_in(own, 1), rows)]
    offset_by = jax.random.randint(jax.random.fold_in(own, 2), (rows, 1), 0, top)
    return jnp.take_along_axis(table, (jnp.arange(top)[None, :] + offset_by) % top, axis=1)


def load_shares(number_of, total, reach, lean, full):
    portions = [(1 << 20) // math.isqrt(rank ** lean) + 1 for rank in range(1, number_of + 1)]
    largest = reach if full else min(reach, max(-(-total // number_of), total * portions[0] // sum(portions)))
    least = 1 if total - largest >= number_of - 1 else 0
    holding, rest = [largest] + [least] * (number_of - 1), total - largest - least * (number_of - 1)
    while rest > 0:
        movable = [i for i in range(1, number_of) if holding[i] < largest] or [i for i in range(1, number_of) if holding[i] < reach]
        whole, remaining = sum([portions[i] for i in movable]), rest
        for i in movable:
            more = min(reach - holding[i], max(1, remaining * portions[i] // whole), rest)
            holding[i] = holding[i] + more
            rest = rest - more
    return np.array(holding)


def centred(own_key, shape, spread, reach, cuts=(), kind=jnp.bfloat16):
    loudness = shard_levels(own_key, shape, cuts, -0.22, 0.18) if cuts else 1.0
    drawn = jax.random.normal(own_key, shape, jnp.float32) * spread * loudness
    return jnp.minimum(jnp.maximum(drawn, -reach), reach).astype(kind)


def gaussian_with(own_key, dims, scale, bound, cuts, heavy, kind=jnp.bfloat16):
    entries = scale * jax.random.normal(own_key, dims, jnp.float32)
    if cuts:
        entries = entries * shard_levels(own_key, dims, cuts, -0.22, 0.18)
    return jnp.clip(raised(entries, jax.random.fold_in(own_key, 3), *heavy), -bound, bound).astype(kind)


def setup_inputs(seed: int = 0, part: int = 0) -> dict:
    keys = jax.random.split(jax.random.key(seed), 15)
    own_keys = jax.random.split(jax.random.fold_in(keys[14], part), 15)
    request_query_rows = draw_request_query_rows(jax.random.fold_in(jax.random.fold_in(keys[14], part), 71), part)
    new_kv = draw_new_kv(jax.random.fold_in(jax.random.fold_in(keys[14], part), 71), part)
    kv_pool = draw_kv_pool(jax.random.fold_in(jax.random.fold_in(keys[14], part), 71), part)
    page_table = jax.vmap(lambda own: jax.random.permutation(own, POOL))(jax.random.split(own_keys[3], N_DEV)).reshape((N_DEV, POOL)).astype(jnp.int32)
    page_count = jax.vmap(lambda own: uneven(own, REQ_DEV, POOL, MAXP, 2))(jax.random.split(own_keys[4], N_DEV)).reshape((N_DEV, REQ_DEV)).astype(jnp.int32)
    last_fill = with_ends(jax.random.randint(own_keys[5], (N_DEV, REQ_DEV), 1, PAGE + 1), jax.random.fold_in(own_keys[5], 1), 1, PAGE).astype(jnp.int32)
    mig_slot = draw_mig_slot(jax.random.fold_in(jax.random.fold_in(keys[14], part), 71), part)
    residual = draw_residual(jax.random.fold_in(jax.random.fold_in(keys[14], part), 71), part)
    norm_gain = jnp.clip(1.0 + 0.18 * jax.random.normal(keys[8], (D,), jnp.float32), 0.1, 1.9)
    route_ids_keys = jax.random.split(jax.random.fold_in(own_keys[9], 1), TOK // REQ_DEV)
    route_ids_turns = jax.random.permutation(jax.random.fold_in(own_keys[9], 3), TOK // REQ_DEV)
    route_ids = jax.vmap(lambda own, number: shared_out(jax.random.fold_in(own_keys[9], 2), own, number, REQ_DEV, EXPERTS, TOPK, MOST, 1))(route_ids_keys, route_ids_turns).reshape((TOK, TOPK))
    route_logit = centred(own_keys[10], (TOK, TOPK), 1.5, 6.0, ((0, 16),))
    w_gate = centred(keys[11], (D, FFW), D ** -0.5, 0.078125, ((1, 16),))
    w_up = centred(keys[12], (D, FFW), D ** -0.5, 0.078125, ((1, 16),))
    w_down = gaussian_with(keys[13], (FFW, D), FFW ** -0.5, 0.1875, ((0, 16),), (0, 1, 16, 2.0))
    return dict(request_query_rows=request_query_rows, new_kv=new_kv, kv_pool=kv_pool, page_table=page_table, page_count=page_count, last_fill=last_fill, mig_slot=mig_slot, residual=residual, norm_gain=norm_gain, route_ids=route_ids, route_logit=route_logit, w_gate=w_gate, w_up=w_up, w_down=w_down)


epsilon = 1e-05

def attend(request_query_rows, incoming_key_value, cache_row_block, length):
    total_row_count = request_query_rows.shape[0]
    query_group_count = QUERY_HEADS // KEY_VALUE_HEADS
    key_row_width = KEY_VALUE_HEADS * HEAD_SIZE
    query_by_group = request_query_rows.astype(jnp.float32).reshape(total_row_count, KEY_VALUE_HEADS, query_group_count, HEAD_SIZE)
    stored_key_rows = cache_row_block[:, :, :key_row_width].astype(jnp.float32).reshape(total_row_count, CACHE_LENGTH, KEY_VALUE_HEADS, HEAD_SIZE)
    stored_value_rows = cache_row_block[:, :, key_row_width:].astype(jnp.float32).reshape(total_row_count, CACHE_LENGTH, KEY_VALUE_HEADS, HEAD_SIZE)
    latest_key = incoming_key_value[:, :key_row_width].astype(jnp.float32).reshape(total_row_count, KEY_VALUE_HEADS, HEAD_SIZE)
    latest_value = incoming_key_value[:, key_row_width:].astype(jnp.float32).reshape(total_row_count, KEY_VALUE_HEADS, HEAD_SIZE)
    score_scale = HEAD_SIZE ** (-0.5)
    past_score = jnp.einsum('rgjd,rlgd->rgjl', query_by_group, stored_key_rows) * score_scale
    own_score = jnp.einsum('rgjd,rgd->rgj', query_by_group, latest_key) * score_scale
    inside = jnp.arange(CACHE_LENGTH, dtype=jnp.int32)[None, :] < length[:, None]
    past_score = jnp.where(inside[:, None, None, :], past_score, -jnp.inf)
    highest = jnp.maximum(lax.optimization_barrier(jnp.max(past_score, axis=-1)), own_score)
    past_exp = jnp.exp(past_score - highest[..., None])
    own_exp = jnp.exp(own_score - highest)
    denominator = lax.optimization_barrier(jnp.sum(past_exp, axis=-1)) + own_exp
    past_weight = lax.optimization_barrier((past_exp / denominator[..., None]).astype(jnp.bfloat16)).astype(jnp.float32)
    own_weight = lax.optimization_barrier((own_exp / denominator).astype(jnp.bfloat16)).astype(jnp.float32)
    mixture = jnp.einsum('rgjl,rlgd->rgjd', past_weight, stored_value_rows)
    mixture = mixture + own_weight[..., None] * latest_value[:, :, None, :]
    return mixture.reshape(total_row_count, QUERY_HEADS * HEAD_SIZE).astype(jnp.bfloat16)

def reference(request_query_rows, new_kv, kv_pool, page_table, page_count, last_fill, mig_slot, residual, norm_gain, route_ids, route_logit, w_gate, w_up, w_down):
    dev_ids = jnp.arange(N_DEV, dtype=jnp.int32)[:, None]
    slot_ids = jnp.arange(REQ_DEV, dtype=jnp.int32)[None, :]
    src_dev = jnp.broadcast_to(dev_ids, (N_DEV, REQ_DEV))
    src_slot = jnp.broadcast_to(slot_ids, (N_DEV, REQ_DEV))
    for bit_index in range(NBITS):
        partner = jnp.bitwise_xor(dev_ids, 1 << bit_index).astype(jnp.int32)
        my_slot = mig_slot[:, bit_index][:, None]
        theirs = mig_slot[partner[:, 0], bit_index][:, None]
        matched = slot_ids == my_slot
        src_dev = jnp.where(matched, partner, src_dev)
        src_slot = jnp.where(matched, theirs, src_slot)
    starts = jnp.cumsum(page_count, axis=1) - page_count
    lengths = (page_count - 1) * PAGE + last_fill
    offsets = jnp.arange(MAXP, dtype=jnp.int32)
    positions = jnp.arange(CACHE_LENGTH, dtype=jnp.int32)

    def one_device(device_index):
        source_dev = src_dev[device_index]
        source_slot = src_slot[device_index]
        global_rows = source_dev * REQ_DEV + source_slot
        page_slots = jnp.clip(starts[source_dev, source_slot][:, None] + offsets[None, :], 0, POOL - 1)
        physical = source_dev[:, None] * POOL + page_table[source_dev[:, None], page_slots]
        blocks = kv_pool[physical].reshape(REQ_DEV, CACHE_LENGTH, KVW)
        length = lengths[source_dev, source_slot]
        inside = positions[None, :] < length[:, None]
        cache_row_block = jnp.where(inside[:, :, None], blocks, jnp.zeros_like(blocks))
        attended = attend(request_query_rows[global_rows], new_kv[global_rows], cache_row_block, length)
        arrived = cache_row_block[mig_slot[device_index]]
        return (attended, arrived)
    attended, arrived = lax.map(one_device, jnp.arange(N_DEV, dtype=jnp.int32))
    attended = attended.reshape(TOK, QW)
    global_all = (src_dev * REQ_DEV + src_slot).reshape(-1)
    hidden_state = residual[global_all].astype(jnp.float32) + lax.optimization_barrier(attended).astype(jnp.float32)
    mean_square = lax.optimization_barrier(jnp.mean(hidden_state * hidden_state, axis=1, keepdims=True))
    normed = (hidden_state * lax.rsqrt(mean_square + epsilon) * norm_gain).astype(jnp.bfloat16)
    gate_proj = jnp.dot(normed, w_gate, preferred_element_type=jnp.float32)
    up_proj = jnp.dot(normed, w_up, preferred_element_type=jnp.float32)
    acts = (jax.nn.silu(gate_proj) * up_proj).astype(jnp.bfloat16)
    summed = jnp.dot(acts, w_down, preferred_element_type=jnp.float32)
    route_probs = jax.nn.softmax(route_logit[global_all].astype(jnp.float32), axis=1)
    route_weight = lax.optimization_barrier(jnp.sum(jnp.where(route_ids[global_all] == 0, route_probs, 0.0), axis=1))
    layer_out = (hidden_state + route_weight[:, None] * summed).astype(jnp.bfloat16)
    arrived_cache = arrived.reshape(N_DEV * NBITS, CACHE_LENGTH, KVW)
    return (layer_out, arrived_cache)
```

```python
import functools

import jax
import jax.numpy as jnp
from jax import lax
from jax.experimental import pallas as pl
from jax.experimental.pallas import tpu as pltpu
from jax.sharding import PartitionSpec as P

KEY_VALUE_HEADS = 8
LANES = 128
NBITS = 3
REQ = 3

epsilon = 1e-05


def flipped(value, bit):
    return value + bit - 2 * bit * ((value // bit) % 2)


def layer_kernel(
    n,
    bits,
    maxp,
    q_ref,
    nkv_ref,
    pool_hbm,
    table,
    counts,
    fills,
    mig,
    res_ref,
    gain_ref,
    ids_ref,
    logit_ref,
    wg_hbm,
    wu_hbm,
    wd_hbm,
    out_ref,
    arr_ref,
    pool,
    cache,
    wg,
    wu,
    wd,
    qs,
    kvs,
    rs,
    route,
    hid_send,
    hid_recv,
    gathered,
    wide,
    rows_x,
    shares,
    rs_send,
    rs_recv,
    fin,
    local_sem,
    cache_send_sem,
    cache_recv_sem,
    hid_send_sem,
    hid_recv_sem,
    ag_send_sem,
    ag_recv_sem,
    rs_send_sem,
    rs_recv_sem,
):
    me = lax.axis_index("dev")
    page = pool.shape[1]
    width = pool.shape[2]
    pool_pages = pool.shape[0]
    chunks = q_ref.shape[1] // LANES
    kvc = nkv_ref.shape[1] // LANES
    group = chunks // KEY_VALUE_HEADS
    key_width = KEY_VALUE_HEADS * LANES
    block = REQ * chunks
    scale = LANES ** (-0.5)

    pool_copy = pltpu.make_async_copy(pool_hbm, pool, local_sem.at[0])
    pool_copy.start()
    weight_copies = [
        pltpu.make_async_copy(src, dst, local_sem.at[1 + i])
        for i, (src, dst) in enumerate(((wg_hbm, wg), (wu_hbm, wu), (wd_hbm, wd)))
    ]
    for copy in weight_copies:
        copy.start()

    barrier = pltpu.get_barrier_semaphore()
    partners = [flipped(me, 1 << k) for k in range(bits)]
    for partner in partners:
        pl.semaphore_signal(
            barrier, inc=1, device_id={"dev": partner}, device_id_type=pl.DeviceIdType.MESH
        )

    pos = 0
    for k in range(bits):
        pos = pos + ((me // (1 << k)) % 2) * (1 << (bits - 1 - k))

    qf = q_ref[...].astype(jnp.float32)
    rf = res_ref[...].astype(jnp.float32)
    for c in range(chunks):
        qs[pl.ds(c, REQ, stride=chunks), :] = qf[:, c * LANES : (c + 1) * LANES]
        rs[pl.ds(c, REQ, stride=chunks), :] = rf[:, c * LANES : (c + 1) * LANES]
    kf = nkv_ref[...].astype(jnp.float32)
    for c in range(kvc):
        kvs[pl.ds(c, REQ, stride=kvc), :] = kf[:, c * LANES : (c + 1) * LANES]
    logits = logit_ref[...].astype(jnp.float32)
    e = jnp.exp(logits - jnp.max(logits, axis=1, keepdims=True))
    probs = e / jnp.sum(e, axis=1, keepdims=True)
    chosen = jnp.sum(jnp.where(ids_ref[...] == 0, probs, 0.0), axis=1, keepdims=True)
    route[...] = jnp.zeros_like(route)
    route[pl.ds(0, REQ), :] = jnp.broadcast_to(chosen, (REQ, LANES))

    def picked(slot, values):
        chosen_value = values[REQ - 1]
        for i in range(REQ - 2, -1, -1):
            chosen_value = jnp.where(slot == i, values[i], chosen_value)
        return chosen_value

    spans = [(counts[0, s] - 1) * page + fills[0, s] for s in range(REQ)]
    firsts = [jnp.int32(0)]
    for s in range(REQ - 1):
        firsts.append(firsts[-1] + counts[0, s])
    slots = [mig[0, b] for b in range(NBITS)]
    lengths = [picked(slot, spans) for slot in slots]
    starts = [picked(slot, firsts) for slot in slots]
    visible = maxp * page
    pool_rows = pool_pages * page
    row = lax.broadcasted_iota(jnp.int32, (visible, LANES), 0)
    row_page = row // page
    lane = lax.broadcasted_iota(jnp.int32, (visible, pool_rows), 1)

    def chooser(b):
        ordinal = row_page + starts[b]
        target = jnp.zeros((visible, LANES), jnp.int32)
        for j in range(pool_pages):
            target = jnp.where(ordinal == j, table[0, j], target)
        target = target * page + (row - row_page * page)
        target = jnp.where(row < lengths[b], target, -1)[:, :1]
        return jnp.where(lane == target, 1.0, 0.0).astype(jnp.bfloat16)

    choosers = [chooser(b) for b in range(NBITS)]

    pool_copy.wait()
    pl.semaphore_wait(barrier, bits)

    cache_copies = {}
    for b in (1, 2, 0):
        cache[b] = jnp.dot(
            choosers[b], pool[...].reshape(pool_rows, width), preferred_element_type=jnp.float32
        ).astype(jnp.bfloat16)
        cache_copies[b] = pltpu.make_async_remote_copy(
            src_ref=cache.at[b],
            dst_ref=arr_ref.at[b],
            send_sem=cache_send_sem.at[b],
            recv_sem=cache_recv_sem.at[b],
            device_id={"dev": partners[b]},
            device_id_type=pl.DeviceIdType.MESH,
        )
        cache_copies[b].start()

    head = lax.broadcasted_iota(jnp.int32, (chunks, LANES), 0)
    position = lax.broadcasted_iota(jnp.int32, (chunks, maxp * page), 1)

    def spread(parts):
        total = parts(0)
        for g in range(1, KEY_VALUE_HEADS):
            total = jnp.where(head >= g * group, parts(g), total)
        return total

    hid_copies = []
    for b in range(NBITS):
        slot = slots[b]
        qrow = picked(slot, [qs[s * chunks : (s + 1) * chunks, :] for s in range(REQ)])
        q16 = qrow.astype(jnp.bfloat16)
        nk, nv = [
            picked(slot, [kvs[pl.ds(s * kvc + at, KEY_VALUE_HEADS), :] for s in range(REQ)])
            for at in (0, KEY_VALUE_HEADS)
        ]
        score = spread(
            lambda g: lax.dot_general(
                q16,
                cache[b, :, g * LANES : (g + 1) * LANES],
                (((1,), (1,)), ((), ())),
                preferred_element_type=jnp.float32,
            )
        )
        new_key = spread(lambda g: jnp.broadcast_to(nk[g : g + 1, :], (chunks, LANES)))
        new_value = spread(lambda g: jnp.broadcast_to(nv[g : g + 1, :], (chunks, LANES)))
        own_score = jnp.sum(qrow * new_key, axis=1, keepdims=True) * scale
        score = jnp.where(position < lengths[b], score * scale, -jnp.inf)
        highest = jnp.maximum(jnp.max(score, axis=1, keepdims=True), own_score)
        past = jnp.exp(score - highest)
        mine = jnp.exp(own_score - highest)
        denominator = jnp.sum(past, axis=1, keepdims=True) + mine
        weight = (past / denominator).astype(jnp.bfloat16)
        own_weight = (mine / denominator).astype(jnp.bfloat16).astype(jnp.float32)
        mixture = spread(
            lambda g: jnp.dot(
                weight,
                cache[b, :, key_width + g * LANES : key_width + (g + 1) * LANES],
                preferred_element_type=jnp.float32,
            )
        )
        attended = (mixture + own_weight * new_value).astype(jnp.bfloat16)
        rest = picked(slot, [rs[s * chunks : (s + 1) * chunks, :] for s in range(REQ)])
        hidden = rest + attended.astype(jnp.float32)
        mean_square = jnp.sum(
            jnp.sum(hidden * hidden, axis=1, keepdims=True), axis=0, keepdims=True
        ) * (1.0 / (chunks * LANES))
        normed = hidden * lax.rsqrt(mean_square + epsilon) * gain_ref[...]
        gathered[pl.ds(pl.multiple_of(pos * block + b * chunks, 16), chunks), :] = normed.astype(
            jnp.bfloat16
        )
        hid_send[b, pl.ds(0, chunks), :] = hidden
        hid_send[b, pl.ds(chunks, 8), :] = jnp.broadcast_to(
            picked(slot, [route[s : s + 1, :] for s in range(REQ)]), (8, LANES)
        )
        copy = pltpu.make_async_remote_copy(
            src_ref=hid_send.at[b],
            dst_ref=hid_recv.at[b],
            send_sem=hid_send_sem.at[b],
            recv_sem=hid_recv_sem.at[b],
            device_id={"dev": partners[b]},
            device_id_type=pl.DeviceIdType.MESH,
        )
        hid_copies.append(copy)

    def widen(first, amount):
        def one(i, carry):
            source = first + i
            for b in range(NBITS):
                target = flipped(source, 1 << (bits - 1 - b))
                wide[pl.ds(pl.multiple_of((target * REQ + b) * chunks, 16), chunks), :] = gathered[
                    pl.ds(pl.multiple_of((source * REQ + b) * chunks, 16), chunks), :
                ].astype(jnp.float32)
            return carry

        lax.fori_loop(0, amount, one, 0)

    ag_copies = []
    for step in range(bits):
        k = bits - 1 - step
        size = 1 << step
        have = (pos // size) * size
        rows = pl.ds(pl.multiple_of(have * block, 16), size * block)
        copy = pltpu.make_async_remote_copy(
            src_ref=gathered.at[rows, :],
            dst_ref=gathered.at[rows, :],
            send_sem=ag_send_sem.at[step],
            recv_sem=ag_recv_sem.at[step],
            device_id={"dev": partners[k]},
            device_id_type=pl.DeviceIdType.MESH,
        )
        copy.start()
        ag_copies.append(copy)
        if step == 0:
            for hid in hid_copies:
                hid.start()
            widen(pos, 1)
        else:
            widen(other, size // 2)
        copy.wait_recv()
        other = flipped(have // size, 1) * size
    widen(other, n // 2)

    count = n * REQ
    for c in range(chunks):
        rows_x[:, c * LANES : (c + 1) * LANES] = wide[pl.ds(c, count, stride=chunks), :].astype(
            jnp.bfloat16
        )
    weight_copies[0].wait()
    weight_copies[1].wait()
    x = rows_x[...]
    gate = jnp.dot(x, wg[...], preferred_element_type=jnp.float32)
    up = jnp.dot(x, wu[...], preferred_element_type=jnp.float32)
    acts = (gate * (1.0 / (1.0 + jnp.exp(-gate))) * up).astype(jnp.bfloat16)
    weight_copies[2].wait()
    piece = 4
    for c in range(0, chunks, piece):
        y = jnp.dot(
            acts, wd[:, c * LANES : (c + piece) * LANES], preferred_element_type=jnp.float32
        )
        for j in range(piece):
            shares[pl.ds(c + j, count, stride=chunks), :] = y[:, j * LANES : (j + 1) * LANES]

    rs_copies = []
    offset = 0
    for k in range(bits):
        half = n >> (k + 1)
        mine_at = (pos // half) * half
        theirs_at = flipped(pos // half, 1) * half
        slab = pl.ds(offset * block, half * block)
        rs_send[slab, :] = shares[
            pl.ds(pl.multiple_of(theirs_at * block, 16), half * block), :
        ].astype(jnp.bfloat16)
        copy = pltpu.make_async_remote_copy(
            src_ref=rs_send.at[slab, :],
            dst_ref=rs_recv.at[slab, :],
            send_sem=rs_send_sem.at[k],
            recv_sem=rs_recv_sem.at[k],
            device_id={"dev": partners[k]},
            device_id_type=pl.DeviceIdType.MESH,
        )
        copy.start()
        rs_copies.append(copy)
        copy.wait_recv()
        keep = pl.ds(pl.multiple_of(mine_at * block, 16), half * block)
        shares[keep, :] = shares[keep, :] + rs_recv[slab, :].astype(jnp.float32)
        offset += half

    done = []
    for b in range(NBITS):
        hid_copies[b].wait_recv()
        summed = shares[pl.ds(pl.multiple_of(pos * block + b * chunks, 16), chunks), :]
        done.append(hid_recv[b, pl.ds(0, chunks), :] + hid_recv[b, pl.ds(chunks, 1), :] * summed)
    for s in range(REQ):
        row = jnp.where(slots[0] == s, done[0], jnp.where(slots[1] == s, done[1], done[2]))
        fin[pl.ds(s * chunks, chunks), :] = row
    for c in range(chunks):
        out_ref[:, c * LANES : (c + 1) * LANES] = fin[pl.ds(c, REQ, stride=chunks), :].astype(
            jnp.bfloat16
        )

    for copy in ag_copies + rs_copies + hid_copies:
        copy.wait_send()
    for b in range(NBITS):
        cache_copies[b].wait()


def on_device(
    request_query_rows,
    new_kv,
    kv_pool,
    page_table,
    page_count,
    last_fill,
    mig_slot,
    residual,
    norm_gain,
    route_ids,
    route_logit,
    w_gate,
    w_up,
    w_down,
):
    n = lax.axis_size("dev")
    bits = n.bit_length() - 1
    maxp = 8
    page, width = kv_pool.shape[1:]
    d = residual.shape[1]
    chunks = d // LANES
    kvc = width // LANES
    rows = n * REQ * chunks
    block = REQ * chunks
    hidden_units = w_down.shape[0]
    vmem = pl.BlockSpec(memory_space=pltpu.VMEM)
    smem = pl.BlockSpec(memory_space=pltpu.SMEM)
    anywhere = pl.BlockSpec(memory_space=pl.ANY)
    f32, bf16 = jnp.float32, jnp.bfloat16
    dma = pltpu.SemaphoreType.DMA
    layer_out, arrived = pl.pallas_call(
        functools.partial(layer_kernel, n, bits, maxp),
        out_shape=(
            jax.ShapeDtypeStruct((REQ, d), bf16),
            jax.ShapeDtypeStruct((NBITS, maxp * page, width), bf16),
        ),
        in_specs=[
            vmem, vmem, anywhere, smem, smem, smem, smem, vmem, vmem, vmem, vmem,
            anywhere, anywhere, anywhere,
        ],
        out_specs=(vmem, anywhere),
        scratch_shapes=[
            pltpu.VMEM(kv_pool.shape, bf16),
            pltpu.VMEM((NBITS, maxp * page, width), bf16),
            pltpu.VMEM(w_gate.shape, bf16),
            pltpu.VMEM(w_up.shape, bf16),
            pltpu.VMEM(w_down.shape, bf16),
            pltpu.VMEM((block, LANES), f32),
            pltpu.VMEM((REQ * kvc, LANES), f32),
            pltpu.VMEM((block, LANES), f32),
            pltpu.VMEM((8, LANES), f32),
            pltpu.VMEM((NBITS, chunks + 8, LANES), f32),
            pltpu.VMEM((NBITS, chunks + 8, LANES), f32),
            pltpu.VMEM((rows, LANES), bf16),
            pltpu.VMEM((rows, LANES), f32),
            pltpu.VMEM((n * REQ, d), bf16),
            pltpu.VMEM((rows, LANES), f32),
            pltpu.VMEM(((n - 1) * block, LANES), bf16),
            pltpu.VMEM(((n - 1) * block, LANES), bf16),
            pltpu.VMEM((block, LANES), f32),
            dma((4,)),
            dma((NBITS,)),
            dma((NBITS,)),
            dma((NBITS,)),
            dma((NBITS,)),
            dma((bits,)),
            dma((bits,)),
            dma((bits,)),
            dma((bits,)),
        ],
        compiler_params=pltpu.CompilerParams(
            collective_id=0, has_side_effects=True, vmem_limit_bytes=56 * 1024 * 1024
        ),
    )(
        request_query_rows,
        new_kv,
        kv_pool,
        page_table,
        page_count,
        last_fill,
        mig_slot,
        residual,
        norm_gain.reshape(chunks, LANES),
        route_ids,
        route_logit,
        w_gate,
        w_up,
        w_down,
    )
    return layer_out, arrived


def solution(mesh):
    rows = P(("groups", "dev"), None)
    pages = P(("groups", "dev"), None, None)
    placed = (rows, rows, pages, rows, rows, rows, rows, rows, P(), rows, rows)
    placed += (P(None, "dev"), P(None, "dev"), P("dev", None))
    return jax.shard_map(
        on_device, mesh=mesh, in_specs=placed, out_specs=(rows, pages), check_vma=False
    )
```

```python
import functools

import jax
import jax.numpy as jnp
from jax import lax
from jax.experimental import pallas as pl
from jax.experimental.pallas import tpu as pltpu
from jax.sharding import PartitionSpec as P

KEY_VALUE_HEADS = 8
LANES = 128
NBITS = 3
REQ = 3
CACHE_CUTS = ((0, 8), (0, 2, 6, 8), (0, 2, 6, 8))
CACHE_PARTS = 3

epsilon = 1e-05


def flipped(value, bit):
    return value + bit - 2 * bit * ((value // bit) % 2)


def layer_kernel(
    n,
    bits,
    maxp,
    q_ref,
    nkv_ref,
    pool_hbm,
    table,
    counts,
    fills,
    mig,
    res_ref,
    gain_ref,
    ids_ref,
    logit_ref,
    wg_hbm,
    wu_hbm,
    wd_hbm,
    out_ref,
    arr_ref,
    pool,
    cache,
    wg,
    wu,
    wd,
    qs,
    kvs,
    rs,
    hid_send,
    hid_recv,
    gathered,
    wide,
    rows_x,
    shares,
    rs_send,
    rs_recv,
    fin,
    local_sem,
    cache_send_sem,
    cache_recv_sem,
    hid_send_sem,
    hid_recv_sem,
    ag_send_sem,
    ag_recv_sem,
    rs_send_sem,
    rs_recv_sem,
):
    me = lax.axis_index("dev")
    page = pool.shape[1]
    width = pool.shape[2]
    pool_pages = pool.shape[0]
    chunks = q_ref.shape[1] // LANES
    kvc = nkv_ref.shape[1] // LANES
    group = chunks // KEY_VALUE_HEADS
    key_width = KEY_VALUE_HEADS * LANES
    block = REQ * chunks
    scale = LANES ** (-0.5)

    pool_copy = pltpu.make_async_copy(pool_hbm, pool, local_sem.at[0])
    pool_copy.start()
    weight_copies = [
        pltpu.make_async_copy(src, dst, local_sem.at[1 + i])
        for i, (src, dst) in enumerate(((wg_hbm, wg), (wu_hbm, wu), (wd_hbm, wd)))
    ]
    for copy in weight_copies:
        copy.start()

    barrier = pltpu.get_barrier_semaphore()
    partners = [flipped(me, 1 << k) for k in range(bits)]
    diagonal = flipped(partners[1], 4)
    for partner in partners + [diagonal]:
        pl.semaphore_signal(
            barrier, inc=1, device_id={"dev": partner}, device_id_type=pl.DeviceIdType.MESH
        )

    pos = 0
    for k in range(bits):
        pos = pos + ((me // (1 << k)) % 2) * (1 << (bits - 1 - k))

    qf = q_ref[...].astype(jnp.float32)
    rf = res_ref[...].astype(jnp.float32)
    for c in range(chunks):
        qs[pl.ds(c, REQ, stride=chunks), :] = qf[:, c * LANES : (c + 1) * LANES]
        rs[pl.ds(c, REQ, stride=chunks), :] = rf[:, c * LANES : (c + 1) * LANES]
    kf = nkv_ref[...].astype(jnp.float32)
    for c in range(kvc):
        kvs[pl.ds(c, REQ, stride=kvc), :] = kf[:, c * LANES : (c + 1) * LANES]
    logits = logit_ref[...].astype(jnp.float32)
    e = jnp.exp(logits - jnp.max(logits, axis=0, keepdims=True))
    probs = e / jnp.sum(e, axis=0, keepdims=True)
    chosen = jnp.sum(jnp.where(ids_ref[...] == 0, probs, 0.0), axis=0, keepdims=True)
    route = [jnp.broadcast_to(chosen[:, s : s + 1], (8, LANES)) for s in range(REQ)]

    def picked(slot, values):
        chosen_value = values[REQ - 1]
        for i in range(REQ - 2, -1, -1):
            chosen_value = jnp.where(slot == i, values[i], chosen_value)
        return chosen_value

    spans = [(counts[0, s] - 1) * page + fills[0, s] for s in range(REQ)]
    firsts = [jnp.int32(0)]
    for s in range(REQ - 1):
        firsts.append(firsts[-1] + counts[0, s])
    slots = [mig[0, b] for b in range(NBITS)]
    lengths = [picked(slot, spans) for slot in slots]
    starts = [picked(slot, firsts) for slot in slots]
    visible = maxp * page
    pool_rows = pool_pages * page
    row = lax.broadcasted_iota(jnp.int32, (visible, LANES), 0)
    row_page = row // page
    lane = lax.broadcasted_iota(jnp.int32, (visible, pool_rows), 1)

    def chooser(b):
        ordinal = row_page + starts[b]
        target = jnp.zeros((visible, LANES), jnp.int32)
        for j in range(pool_pages):
            target = jnp.where(ordinal == j, table[0, j], target)
        target = target * page + (row - row_page * page)
        target = jnp.where(row < lengths[b], target, -1)[:, :1]
        return jnp.where(lane == target, 1.0, 0.0).astype(jnp.bfloat16)

    choosers = [chooser(b) for b in range(NBITS)]

    pool_copy.wait()
    pl.semaphore_wait(barrier, bits + 1)

    cache_copies = {}
    for b in (1, 2, 0):
        cache[b] = jnp.dot(
            choosers[b], pool[...].reshape(pool_rows, width), preferred_element_type=jnp.float32
        ).astype(jnp.bfloat16)
        cuts = CACHE_CUTS[b]
        for part in range(len(cuts) - 1):
            rows = pl.ds(cuts[part] * page, (cuts[part + 1] - cuts[part]) * page)
            cache_copies[b, part] = pltpu.make_async_remote_copy(
                src_ref=cache.at[b, rows],
                dst_ref=arr_ref.at[b, rows],
                send_sem=cache_send_sem.at[b, part],
                recv_sem=cache_recv_sem.at[b, part],
                device_id={"dev": partners[b]},
                device_id_type=pl.DeviceIdType.MESH,
            )
        cache_copies[b, 0].start()

    def start_caches(part):
        for b in (1, 2, 0):
            if (b, part) in cache_copies:
                cache_copies[b, part].start()

    head = lax.broadcasted_iota(jnp.int32, (chunks, LANES), 0)
    position = lax.broadcasted_iota(jnp.int32, (chunks, maxp * page), 1)

    def spread(parts):
        total = parts(0)
        for g in range(1, KEY_VALUE_HEADS):
            total = jnp.where(head >= g * group, parts(g), total)
        return total

    hid_copies = []
    for b in range(NBITS):
        slot = slots[b]
        qrow = picked(slot, [qs[s * chunks : (s + 1) * chunks, :] for s in range(REQ)])
        q16 = qrow.astype(jnp.bfloat16)
        nk, nv = [
            picked(slot, [kvs[pl.ds(s * kvc + at, KEY_VALUE_HEADS), :] for s in range(REQ)])
            for at in (0, KEY_VALUE_HEADS)
        ]
        score = spread(
            lambda g: lax.dot_general(
                q16,
                cache[b, :, g * LANES : (g + 1) * LANES],
                (((1,), (1,)), ((), ())),
                preferred_element_type=jnp.float32,
            )
        )
        new_key = spread(lambda g: jnp.broadcast_to(nk[g : g + 1, :], (chunks, LANES)))
        new_value = spread(lambda g: jnp.broadcast_to(nv[g : g + 1, :], (chunks, LANES)))
        own_score = jnp.sum(qrow * new_key, axis=1, keepdims=True) * scale
        score = jnp.where(position < lengths[b], score * scale, -jnp.inf)
        highest = jnp.maximum(jnp.max(score, axis=1, keepdims=True), own_score)
        past = jnp.exp(score - highest)
        mine = jnp.exp(own_score - highest)
        denominator = jnp.sum(past, axis=1, keepdims=True) + mine
        weight = (past / denominator).astype(jnp.bfloat16)
        own_weight = (mine / denominator).astype(jnp.bfloat16).astype(jnp.float32)
        mixture = spread(
            lambda g: jnp.dot(
                weight,
                cache[b, :, key_width + g * LANES : key_width + (g + 1) * LANES],
                preferred_element_type=jnp.float32,
            )
        )
        attended = (mixture + own_weight * new_value).astype(jnp.bfloat16)
        rest = picked(slot, [rs[s * chunks : (s + 1) * chunks, :] for s in range(REQ)])
        hidden = rest + attended.astype(jnp.float32)
        mean_square = jnp.sum(
            jnp.sum(hidden * hidden, axis=1, keepdims=True), axis=0, keepdims=True
        ) * (1.0 / (chunks * LANES))
        normed = hidden * lax.rsqrt(mean_square + epsilon) * gain_ref[...]
        gathered[pl.ds(pl.multiple_of(pos * block + b * chunks, 16), chunks), :] = normed.astype(
            jnp.bfloat16
        )
        hid_send[b, pl.ds(0, chunks), :] = hidden
        hid_send[b, pl.ds(chunks, 8), :] = picked(slot, route)
        copy = pltpu.make_async_remote_copy(
            src_ref=hid_send.at[b],
            dst_ref=hid_recv.at[b],
            send_sem=hid_send_sem.at[b],
            recv_sem=hid_recv_sem.at[b],
            device_id={"dev": partners[b]},
            device_id_type=pl.DeviceIdType.MESH,
        )
        hid_copies.append(copy)

    def widen(first, amount):
        def one(i, carry):
            source = first + i
            for b in range(NBITS):
                target = flipped(source, 1 << (bits - 1 - b))
                wide[pl.ds(pl.multiple_of((target * REQ + b) * chunks, 16), chunks), :] = gathered[
                    pl.ds(pl.multiple_of((source * REQ + b) * chunks, 16), chunks), :
                ].astype(jnp.float32)
            return carry

        lax.fori_loop(0, amount, one, 0)

    def remote(src, dst, send, recv, index, device):
        copy = pltpu.make_async_remote_copy(
            src_ref=src,
            dst_ref=dst,
            send_sem=send.at[index],
            recv_sem=recv.at[index],
            device_id={"dev": device},
            device_id_type=pl.DeviceIdType.MESH,
        )
        copy.start()
        return copy

    def at(first, amount):
        return pl.ds(pl.multiple_of(first * block, 16), amount * block)

    def gather_to(index, first, amount, device):
        rows = gathered.at[at(first, amount), :]
        copy = remote(rows, rows, ag_send_sem, ag_recv_sem, index, device)
        sends.append(copy)
        return copy

    sends = []
    quarter = n // 8
    near, beside = partners[2], partners[1]
    core = [gather_to(0, pos, 1, partners[0])]
    core_from = [(flipped(pos, n // 2), 1)]
    size = 1
    for step in range(bits - 3):
        have = (pos // size) * size
        other = flipped(pos // size, 1) * size
        copy = gather_to(1 + step, have, size, partners[bits - 1 - step])
        if step == 0:
            for hid in hid_copies:
                hid.start()
            widen(pos, 1)
        copy.wait_recv()
        core.append(gather_to(bits + step, other, size, partners[0]))
        core_from.append((flipped(other, n // 2), size))
        widen(other, size)
        size *= 2
    have = (pos // quarter) * quarter
    next_at = flipped(have, quarter)
    beside_at = flipped(have, 2 * quarter)
    cross_at = flipped(next_at, 2 * quarter)
    last = 2 * bits
    arriving = [
        (gather_to(last, have, quarter, diagonal), cross_at),
        (gather_to(last + 1, have, quarter, beside), beside_at),
        (gather_to(last + 2, have, quarter, near), next_at),
    ]
    for (first, amount), copy in zip(core_from, core):
        copy.wait_recv()
        widen(first, amount)
    core = []
    for i, (copy, where) in enumerate(reversed(arriving)):
        copy.wait_recv()
        core.append((gather_to(last + 3 + i, where, quarter, partners[0]), flipped(where, n // 2)))
        widen(where, quarter)
    start_caches(1)
    for copy, where in core:
        copy.wait_recv()
        widen(where, quarter)

    count = n * REQ
    for c in range(chunks):
        rows_x[:, c * LANES : (c + 1) * LANES] = wide[pl.ds(c, count, stride=chunks), :].astype(
            jnp.bfloat16
        )
    weight_copies[0].wait()
    weight_copies[1].wait()
    x = rows_x[...]
    gate = jnp.dot(x, wg[...], preferred_element_type=jnp.float32)
    up = jnp.dot(x, wu[...], preferred_element_type=jnp.float32)
    acts = (gate * (1.0 / (1.0 + jnp.exp(-gate))) * up).astype(jnp.bfloat16)
    weight_copies[2].wait()
    piece = 4
    for c in range(0, chunks, piece):
        y = jnp.dot(
            acts, wd[:, c * LANES : (c + piece) * LANES], preferred_element_type=jnp.float32
        )
        for j in range(piece):
            shares[pl.ds(c + j, count, stride=chunks), :] = y[:, j * LANES : (j + 1) * LANES]

    def cast(first, amount, slot):
        slab = pl.ds(slot * block, amount * block)
        rs_send[slab, :] = shares[at(first, amount), :].astype(jnp.bfloat16)

    def scatter_to(index, slot, amount, device):
        slab = pl.ds(slot * block, amount * block)
        copy = remote(
            rs_send.at[slab, :], rs_recv.at[slab, :], rs_send_sem, rs_recv_sem, index, device
        )
        sends.append(copy)
        return copy

    def arrived_rows(slot, amount):
        return rs_recv[pl.ds(slot * block, amount * block), :].astype(jnp.float32)

    half = n // 2
    cast(flipped(pos // half, 1) * half, half, 0)
    copy = scatter_to(0, 0, half, partners[0])
    copy.wait_recv()
    base = (pos // half) * half
    slot = half
    arriving = []
    for i, (where, device) in enumerate(
        ((cross_at, diagonal), (beside_at, beside), (next_at, near))
    ):
        from_core = rs_recv[at(where - base, quarter), :].astype(jnp.float32)
        slab = pl.ds(slot * block, quarter * block)
        rs_send[slab, :] = (shares[at(where, quarter), :] + from_core).astype(jnp.bfloat16)
        arriving.append((scatter_to(1 + i, slot, quarter, device), slot))
        slot += quarter
    keep = at(have, quarter)
    shares[keep, :] = shares[keep, :] + rs_recv[at(have - base, quarter), :].astype(jnp.float32)
    for copy, _ in arriving:
        copy.wait_recv()
    start_caches(2)
    total = shares[keep, :]
    for _, where in arriving:
        total = total + arrived_rows(where, quarter)
    shares[keep, :] = total
    for k in range(3, bits):
        half = n >> (k + 1)
        mine_at = (pos // half) * half
        cast(flipped(pos // half, 1) * half, half, slot)
        copy = scatter_to(1 + k, slot, half, partners[k])
        copy.wait_recv()
        shares[at(mine_at, half), :] = shares[at(mine_at, half), :] + arrived_rows(slot, half)
        slot += half

    done = []
    for b in range(NBITS):
        hid_copies[b].wait_recv()
        summed = shares[pl.ds(pl.multiple_of(pos * block + b * chunks, 16), chunks), :]
        done.append(hid_recv[b, pl.ds(0, chunks), :] + hid_recv[b, pl.ds(chunks, 1), :] * summed)
    for s in range(REQ):
        row = jnp.where(slots[0] == s, done[0], jnp.where(slots[1] == s, done[1], done[2]))
        fin[pl.ds(s * chunks, chunks), :] = row
    for c in range(chunks):
        out_ref[:, c * LANES : (c + 1) * LANES] = fin[pl.ds(c, REQ, stride=chunks), :].astype(
            jnp.bfloat16
        )

    for copy in sends + hid_copies:
        copy.wait_send()
    for copy in cache_copies.values():
        copy.wait()


def on_device(
    request_query_rows,
    new_kv,
    kv_pool,
    page_table,
    page_count,
    last_fill,
    mig_slot,
    residual,
    norm_gain,
    route_ids,
    route_logit,
    w_gate,
    w_up,
    w_down,
):
    n = lax.axis_size("dev")
    bits = n.bit_length() - 1
    maxp = 8
    page, width = kv_pool.shape[1:]
    d = residual.shape[1]
    chunks = d // LANES
    kvc = width // LANES
    rows = n * REQ * chunks
    block = REQ * chunks
    hidden_units = w_down.shape[0]
    vmem = pl.BlockSpec(memory_space=pltpu.VMEM)
    smem = pl.BlockSpec(memory_space=pltpu.SMEM)
    anywhere = pl.BlockSpec(memory_space=pl.ANY)
    f32, bf16 = jnp.float32, jnp.bfloat16
    dma = pltpu.SemaphoreType.DMA
    layer_out, arrived = pl.pallas_call(
        functools.partial(layer_kernel, n, bits, maxp),
        out_shape=(
            jax.ShapeDtypeStruct((REQ, d), bf16),
            jax.ShapeDtypeStruct((NBITS, maxp * page, width), bf16),
        ),
        in_specs=[
            vmem, vmem, anywhere, smem, smem, smem, smem, vmem, vmem, vmem, vmem,
            anywhere, anywhere, anywhere,
        ],
        out_specs=(vmem, anywhere),
        scratch_shapes=[
            pltpu.VMEM(kv_pool.shape, bf16),
            pltpu.VMEM((NBITS, maxp * page, width), bf16),
            pltpu.VMEM(w_gate.shape, bf16),
            pltpu.VMEM(w_up.shape, bf16),
            pltpu.VMEM(w_down.shape, bf16),
            pltpu.VMEM((block, LANES), f32),
            pltpu.VMEM((REQ * kvc, LANES), f32),
            pltpu.VMEM((block, LANES), f32),
            pltpu.VMEM((NBITS, chunks + 8, LANES), f32),
            pltpu.VMEM((NBITS, chunks + 8, LANES), f32),
            pltpu.VMEM((rows, LANES), bf16),
            pltpu.VMEM((rows, LANES), f32),
            pltpu.VMEM((n * REQ, d), bf16),
            pltpu.VMEM((rows, LANES), f32),
            pltpu.VMEM(((n - 1) * block, LANES), bf16),
            pltpu.VMEM(((n - 1) * block, LANES), bf16),
            pltpu.VMEM((block, LANES), f32),
            dma((4,)),
            dma((NBITS, CACHE_PARTS)),
            dma((NBITS, CACHE_PARTS)),
            dma((NBITS,)),
            dma((NBITS,)),
            dma((2 * bits + 6,)),
            dma((2 * bits + 6,)),
            dma((bits + 1,)),
            dma((bits + 1,)),
        ],
        compiler_params=pltpu.CompilerParams(
            collective_id=0, has_side_effects=True, vmem_limit_bytes=56 * 1024 * 1024
        ),
    )(
        request_query_rows,
        new_kv,
        kv_pool,
        page_table,
        page_count,
        last_fill,
        mig_slot,
        residual,
        norm_gain.reshape(chunks, LANES),
        route_ids.T,
        route_logit.T,
        w_gate,
        w_up,
        w_down,
    )
    return layer_out, arrived


def solution(mesh):
    rows = P(("groups", "dev"), None)
    pages = P(("groups", "dev"), None, None)
    placed = (rows, rows, pages, rows, rows, rows, rows, rows, P(), rows, rows)
    placed += (P(None, "dev"), P(None, "dev"), P("dev", None))
    return jax.shard_map(
        on_device, mesh=mesh, in_specs=placed, out_specs=(rows, pages), check_vma=False
    )
```

```python
import functools

import jax
import jax.numpy as jnp
from jax import lax
from jax.experimental import pallas as pl
from jax.experimental.pallas import tpu as pltpu
from jax.sharding import PartitionSpec as P

KEY_VALUE_HEADS = 8
LANES = 128
NBITS = 3
REQ = 3
CACHE_CUTS = ((0, 8), (0, 2, 6, 8), (0, 2, 6, 8))
CACHE_PARTS = 3

epsilon = 1e-05


def flipped(value, bit):
    return value + bit - 2 * bit * ((value // bit) % 2)


def layer_kernel(
    n,
    bits,
    maxp,
    q_ref,
    nkv_ref,
    pool_hbm,
    table,
    counts,
    fills,
    mig,
    res_ref,
    gain_ref,
    ids_ref,
    logit_ref,
    wg_hbm,
    wu_hbm,
    wd_hbm,
    out_ref,
    arr_ref,
    pool,
    cache,
    wg,
    wu,
    wd,
    qs,
    kvs,
    rs,
    hid_send,
    hid_recv,
    gathered,
    wide,
    rows_x,
    shares,
    rs_send,
    rs_recv,
    fin,
    local_sem,
    cache_send_sem,
    cache_recv_sem,
    hid_send_sem,
    hid_recv_sem,
    ag_send_sem,
    ag_recv_sem,
    rs_send_sem,
    rs_recv_sem,
):
    me = lax.axis_index("dev")
    page = pool.shape[1]
    width = pool.shape[2]
    pool_pages = pool.shape[0]
    chunks = q_ref.shape[1] // LANES
    kvc = nkv_ref.shape[1] // LANES
    group = chunks // KEY_VALUE_HEADS
    key_width = KEY_VALUE_HEADS * LANES
    block = REQ * chunks
    scale = LANES ** (-0.5)

    pool_copy = pltpu.make_async_copy(pool_hbm, pool, local_sem.at[0])
    pool_copy.start()
    weight_copies = [
        pltpu.make_async_copy(src, dst, local_sem.at[1 + i])
        for i, (src, dst) in enumerate(((wg_hbm, wg), (wu_hbm, wu), (wd_hbm, wd)))
    ]
    for copy in weight_copies:
        copy.start()

    barrier = pltpu.get_barrier_semaphore()
    partners = [flipped(me, 1 << k) for k in range(bits)]
    diagonal = flipped(partners[1], 4)
    for partner in partners + [diagonal]:
        pl.semaphore_signal(
            barrier, inc=1, device_id={"dev": partner}, device_id_type=pl.DeviceIdType.MESH
        )

    pos = 0
    for k in range(bits):
        pos = pos + ((me // (1 << k)) % 2) * (1 << (bits - 1 - k))

    qf = q_ref[...].astype(jnp.float32)
    rf = res_ref[...].astype(jnp.float32)
    for c in range(chunks):
        qs[pl.ds(c, REQ, stride=chunks), :] = qf[:, c * LANES : (c + 1) * LANES]
        rs[pl.ds(c, REQ, stride=chunks), :] = rf[:, c * LANES : (c + 1) * LANES]
    kf = nkv_ref[...].astype(jnp.float32)
    for c in range(kvc):
        kvs[pl.ds(c, REQ, stride=kvc), :] = kf[:, c * LANES : (c + 1) * LANES]
    logits = logit_ref[...].astype(jnp.float32)
    e = jnp.exp(logits - jnp.max(logits, axis=0, keepdims=True))
    probs = e / jnp.sum(e, axis=0, keepdims=True)
    chosen = jnp.sum(jnp.where(ids_ref[...] == 0, probs, 0.0), axis=0, keepdims=True)
    route = [jnp.broadcast_to(chosen[:, s : s + 1], (8, LANES)) for s in range(REQ)]

    def picked(slot, values):
        chosen_value = values[REQ - 1]
        for i in range(REQ - 2, -1, -1):
            chosen_value = jnp.where(slot == i, values[i], chosen_value)
        return chosen_value

    spans = [(counts[0, s] - 1) * page + fills[0, s] for s in range(REQ)]
    firsts = [jnp.int32(0)]
    for s in range(REQ - 1):
        firsts.append(firsts[-1] + counts[0, s])
    slots = [mig[0, b] for b in range(NBITS)]
    lengths = [picked(slot, spans) for slot in slots]
    starts = [picked(slot, firsts) for slot in slots]
    visible = maxp * page
    pool_rows = pool_pages * page
    row = lax.broadcasted_iota(jnp.int32, (visible, LANES), 0)
    row_page = row // page
    lane = lax.broadcasted_iota(jnp.int32, (visible, pool_rows), 1)

    def chooser(b):
        ordinal = row_page + starts[b]
        target = jnp.zeros((visible, LANES), jnp.int32)
        for j in range(pool_pages):
            target = jnp.where(ordinal == j, table[0, j], target)
        target = target * page + (row - row_page * page)
        target = jnp.where(row < lengths[b], target, -1)[:, :1]
        return jnp.where(lane == target, 1.0, 0.0).astype(jnp.bfloat16)

    choosers = [chooser(b) for b in range(NBITS)]

    pool_copy.wait()
    pl.semaphore_wait(barrier, bits + 1)

    cache_copies = {}
    for b in (1, 2, 0):
        cache[b] = jnp.dot(
            choosers[b], pool[...].reshape(pool_rows, width), preferred_element_type=jnp.float32
        ).astype(jnp.bfloat16)
        cuts = CACHE_CUTS[b]
        for part in range(len(cuts) - 1):
            rows = pl.ds(cuts[part] * page, (cuts[part + 1] - cuts[part]) * page)
            cache_copies[b, part] = pltpu.make_async_remote_copy(
                src_ref=cache.at[b, rows],
                dst_ref=arr_ref.at[b, rows],
                send_sem=cache_send_sem.at[b, part],
                recv_sem=cache_recv_sem.at[b, part],
                device_id={"dev": partners[b]},
                device_id_type=pl.DeviceIdType.MESH,
            )
        cache_copies[b, 0].start()

    def start_caches(part):
        for b in (1, 2, 0):
            if (b, part) in cache_copies:
                cache_copies[b, part].start()

    head = lax.broadcasted_iota(jnp.int32, (chunks, LANES), 0)
    position = lax.broadcasted_iota(jnp.int32, (chunks, maxp * page), 1)

    def spread(parts):
        total = parts(0)
        for g in range(1, KEY_VALUE_HEADS):
            total = jnp.where(head >= g * group, parts(g), total)
        return total

    hid_copies = []
    for b in range(NBITS):
        slot = slots[b]
        qrow = picked(slot, [qs[s * chunks : (s + 1) * chunks, :] for s in range(REQ)])
        q16 = qrow.astype(jnp.bfloat16)
        nk, nv = [
            picked(slot, [kvs[pl.ds(s * kvc + at, KEY_VALUE_HEADS), :] for s in range(REQ)])
            for at in (0, KEY_VALUE_HEADS)
        ]
        score = spread(
            lambda g: lax.dot_general(
                q16,
                cache[b, :, g * LANES : (g + 1) * LANES],
                (((1,), (1,)), ((), ())),
                preferred_element_type=jnp.float32,
            )
        )
        new_key = spread(lambda g: jnp.broadcast_to(nk[g : g + 1, :], (chunks, LANES)))
        new_value = spread(lambda g: jnp.broadcast_to(nv[g : g + 1, :], (chunks, LANES)))
        own_score = jnp.sum(qrow * new_key, axis=1, keepdims=True) * scale
        score = jnp.where(position < lengths[b], score * scale, -jnp.inf)
        highest = jnp.maximum(jnp.max(score, axis=1, keepdims=True), own_score)
        past = jnp.exp(score - highest)
        mine = jnp.exp(own_score - highest)
        denominator = jnp.sum(past, axis=1, keepdims=True) + mine
        weight = (past / denominator).astype(jnp.bfloat16)
        own_weight = (mine / denominator).astype(jnp.bfloat16).astype(jnp.float32)
        mixture = spread(
            lambda g: jnp.dot(
                weight,
                cache[b, :, key_width + g * LANES : key_width + (g + 1) * LANES],
                preferred_element_type=jnp.float32,
            )
        )
        attended = (mixture + own_weight * new_value).astype(jnp.bfloat16)
        rest = picked(slot, [rs[s * chunks : (s + 1) * chunks, :] for s in range(REQ)])
        hidden = rest + attended.astype(jnp.float32)
        mean_square = jnp.sum(
            jnp.sum(hidden * hidden, axis=1, keepdims=True), axis=0, keepdims=True
        ) * (1.0 / (chunks * LANES))
        normed = hidden * lax.rsqrt(mean_square + epsilon) * gain_ref[...]
        gathered[pl.ds(pl.multiple_of(pos * block + b * chunks, 16), chunks), :] = normed.astype(
            jnp.bfloat16
        )
        hid_send[b, pl.ds(0, chunks), :] = hidden
        hid_send[b, pl.ds(chunks, 8), :] = picked(slot, route)
        copy = pltpu.make_async_remote_copy(
            src_ref=hid_send.at[b],
            dst_ref=hid_recv.at[b],
            send_sem=hid_send_sem.at[b],
            recv_sem=hid_recv_sem.at[b],
            device_id={"dev": partners[b]},
            device_id_type=pl.DeviceIdType.MESH,
        )
        hid_copies.append(copy)

    def widen(first, amount):
        def one(i, carry):
            source = first + i
            for b in range(NBITS):
                target = flipped(source, 1 << (bits - 1 - b))
                wide[pl.ds(pl.multiple_of((target * REQ + b) * chunks, 16), chunks), :] = gathered[
                    pl.ds(pl.multiple_of((source * REQ + b) * chunks, 16), chunks), :
                ].astype(jnp.float32)
            return carry

        lax.fori_loop(0, amount, one, 0)

    def remote(src, dst, send, recv, index, device):
        copy = pltpu.make_async_remote_copy(
            src_ref=src,
            dst_ref=dst,
            send_sem=send.at[index],
            recv_sem=recv.at[index],
            device_id={"dev": device},
            device_id_type=pl.DeviceIdType.MESH,
        )
        copy.start()
        return copy

    def at(first, amount):
        return pl.ds(pl.multiple_of(first * block, 16), amount * block)

    def gather_to(index, first, amount, device):
        rows = gathered.at[at(first, amount), :]
        copy = remote(rows, rows, ag_send_sem, ag_recv_sem, index, device)
        sends.append(copy)
        return copy

    sends = []
    quarter = n // 8
    near, beside = partners[2], partners[1]
    core = [gather_to(0, pos, 1, partners[0])]
    core_from = [(flipped(pos, n // 2), 1)]
    size = 1
    for step in range(bits - 3):
        have = (pos // size) * size
        other = flipped(pos // size, 1) * size
        copy = gather_to(1 + step, have, size, partners[bits - 1 - step])
        if step == 0:
            for hid in hid_copies:
                hid.start()
            widen(pos, 1)
        copy.wait_recv()
        core.append(gather_to(bits + step, other, size, partners[0]))
        core_from.append((flipped(other, n // 2), size))
        widen(other, size)
        size *= 2
    have = (pos // quarter) * quarter
    next_at = flipped(have, quarter)
    beside_at = flipped(have, 2 * quarter)
    cross_at = flipped(next_at, 2 * quarter)
    last = 2 * bits
    arriving = [
        (gather_to(last, have, quarter, diagonal), cross_at),
        (gather_to(last + 1, have, quarter, beside), beside_at),
        (gather_to(last + 2, have, quarter, near), next_at),
    ]
    for (first, amount), copy in zip(core_from, core):
        copy.wait_recv()
        widen(first, amount)
    core = []
    for i, (copy, where) in enumerate(reversed(arriving)):
        copy.wait_recv()
        core.append((gather_to(last + 3 + i, where, quarter, partners[0]), flipped(where, n // 2)))
        widen(where, quarter)
    start_caches(1)
    for copy, where in core:
        copy.wait_recv()
        widen(where, quarter)

    count = n * REQ
    for c in range(chunks):
        rows_x[:, c * LANES : (c + 1) * LANES] = wide[pl.ds(c, count, stride=chunks), :].astype(
            jnp.bfloat16
        )
    weight_copies[0].wait()
    weight_copies[1].wait()
    x = rows_x[...]
    gate = jnp.dot(x, wg[...], preferred_element_type=jnp.float32)
    up = jnp.dot(x, wu[...], preferred_element_type=jnp.float32)
    acts = (gate * (1.0 / (1.0 + jnp.exp(-gate))) * up).astype(jnp.bfloat16)
    weight_copies[2].wait()
    wide[pl.ds(0, count), :] = acts.astype(jnp.float32)
    piece = 4

    def share_rows(first, amount):
        some = wide[pl.ds(pl.multiple_of(first * REQ, 8), amount * REQ), :].astype(jnp.bfloat16)
        for c in range(0, chunks, piece):
            y = jnp.dot(
                some, wd[:, c * LANES : (c + piece) * LANES], preferred_element_type=jnp.float32
            )
            for j in range(piece):
                to = pl.ds(first * block + (c + j), amount * REQ, stride=chunks)
                shares[to, :] = y[:, j * LANES : (j + 1) * LANES]

    def cast(first, amount, slot):
        slab = pl.ds(slot * block, amount * block)
        rs_send[slab, :] = shares[at(first, amount), :].astype(jnp.bfloat16)

    def scatter_to(index, slot, amount, device):
        slab = pl.ds(slot * block, amount * block)
        copy = remote(
            rs_send.at[slab, :], rs_recv.at[slab, :], rs_send_sem, rs_recv_sem, index, device
        )
        sends.append(copy)
        return copy

    def arrived_rows(slot, amount):
        return rs_recv[pl.ds(slot * block, amount * block), :].astype(jnp.float32)

    half = n // 2
    share_rows(flipped(pos // half, 1) * half, half)
    cast(flipped(pos // half, 1) * half, half, 0)
    copy = scatter_to(0, 0, half, partners[0])
    share_rows((pos // half) * half, half)
    copy.wait_recv()
    base = (pos // half) * half
    slot = half
    arriving = []
    for i, (where, device) in enumerate(
        ((cross_at, diagonal), (beside_at, beside), (next_at, near))
    ):
        from_core = rs_recv[at(where - base, quarter), :].astype(jnp.float32)
        slab = pl.ds(slot * block, quarter * block)
        rs_send[slab, :] = (shares[at(where, quarter), :] + from_core).astype(jnp.bfloat16)
        arriving.append((scatter_to(1 + i, slot, quarter, device), slot))
        slot += quarter
    keep = at(have, quarter)
    shares[keep, :] = shares[keep, :] + rs_recv[at(have - base, quarter), :].astype(jnp.float32)
    for copy, _ in arriving:
        copy.wait_recv()
    start_caches(2)
    total = shares[keep, :]
    for _, where in arriving:
        total = total + arrived_rows(where, quarter)
    shares[keep, :] = total
    for k in range(3, bits):
        half = n >> (k + 1)
        mine_at = (pos // half) * half
        cast(flipped(pos // half, 1) * half, half, slot)
        copy = scatter_to(1 + k, slot, half, partners[k])
        copy.wait_recv()
        shares[at(mine_at, half), :] = shares[at(mine_at, half), :] + arrived_rows(slot, half)
        slot += half

    done = []
    for b in range(NBITS):
        hid_copies[b].wait_recv()
        summed = shares[pl.ds(pl.multiple_of(pos * block + b * chunks, 16), chunks), :]
        done.append(hid_recv[b, pl.ds(0, chunks), :] + hid_recv[b, pl.ds(chunks, 1), :] * summed)
    for s in range(REQ):
        row = jnp.where(slots[0] == s, done[0], jnp.where(slots[1] == s, done[1], done[2]))
        fin[pl.ds(s * chunks, chunks), :] = row
    for c in range(chunks):
        out_ref[:, c * LANES : (c + 1) * LANES] = fin[pl.ds(c, REQ, stride=chunks), :].astype(
            jnp.bfloat16
        )

    for copy in sends + hid_copies:
        copy.wait_send()
    for copy in cache_copies.values():
        copy.wait()


def on_device(
    request_query_rows,
    new_kv,
    kv_pool,
    page_table,
    page_count,
    last_fill,
    mig_slot,
    residual,
    norm_gain,
    route_ids,
    route_logit,
    w_gate,
    w_up,
    w_down,
):
    n = lax.axis_size("dev")
    bits = n.bit_length() - 1
    maxp = 8
    page, width = kv_pool.shape[1:]
    d = residual.shape[1]
    chunks = d // LANES
    kvc = width // LANES
    rows = n * REQ * chunks
    block = REQ * chunks
    hidden_units = w_down.shape[0]
    vmem = pl.BlockSpec(memory_space=pltpu.VMEM)
    smem = pl.BlockSpec(memory_space=pltpu.SMEM)
    anywhere = pl.BlockSpec(memory_space=pl.ANY)
    f32, bf16 = jnp.float32, jnp.bfloat16
    dma = pltpu.SemaphoreType.DMA
    layer_out, arrived = pl.pallas_call(
        functools.partial(layer_kernel, n, bits, maxp),
        out_shape=(
            jax.ShapeDtypeStruct((REQ, d), bf16),
            jax.ShapeDtypeStruct((NBITS, maxp * page, width), bf16),
        ),
        in_specs=[
            vmem, vmem, anywhere, smem, smem, smem, smem, vmem, vmem, vmem, vmem,
            anywhere, anywhere, anywhere,
        ],
        out_specs=(vmem, anywhere),
        scratch_shapes=[
            pltpu.VMEM(kv_pool.shape, bf16),
            pltpu.VMEM((NBITS, maxp * page, width), bf16),
            pltpu.VMEM(w_gate.shape, bf16),
            pltpu.VMEM(w_up.shape, bf16),
            pltpu.VMEM(w_down.shape, bf16),
            pltpu.VMEM((block, LANES), f32),
            pltpu.VMEM((REQ * kvc, LANES), f32),
            pltpu.VMEM((block, LANES), f32),
            pltpu.VMEM((NBITS, chunks + 8, LANES), f32),
            pltpu.VMEM((NBITS, chunks + 8, LANES), f32),
            pltpu.VMEM((rows, LANES), bf16),
            pltpu.VMEM((rows, LANES), f32),
            pltpu.VMEM((n * REQ, d), bf16),
            pltpu.VMEM((rows, LANES), f32),
            pltpu.VMEM(((n - 1) * block, LANES), bf16),
            pltpu.VMEM(((n - 1) * block, LANES), bf16),
            pltpu.VMEM((block, LANES), f32),
            dma((4,)),
            dma((NBITS, CACHE_PARTS)),
            dma((NBITS, CACHE_PARTS)),
            dma((NBITS,)),
            dma((NBITS,)),
            dma((2 * bits + 6,)),
            dma((2 * bits + 6,)),
            dma((bits + 1,)),
            dma((bits + 1,)),
        ],
        compiler_params=pltpu.CompilerParams(
            collective_id=0, has_side_effects=True, vmem_limit_bytes=56 * 1024 * 1024
        ),
    )(
        request_query_rows,
        new_kv,
        kv_pool,
        page_table,
        page_count,
        last_fill,
        mig_slot,
        residual,
        norm_gain.reshape(chunks, LANES),
        route_ids.T,
        route_logit.T,
        w_gate,
        w_up,
        w_down,
    )
    return finish(layer_out, arrived)


def finish_kernel(layer_in, arrived_in, layer_out, arrived_out):
    layer_out[...] = layer_in[...]
    arrived_out[...] = arrived_in[...]


def finish(layer, arrived):
    flat = pl.BlockSpec(layer.shape, lambda b: (0, 0))
    one = pl.BlockSpec((1,) + arrived.shape[1:], lambda b: (b, 0, 0))
    return pl.pallas_call(
        finish_kernel,
        grid=(arrived.shape[0],),
        out_shape=(
            jax.ShapeDtypeStruct(layer.shape, layer.dtype),
            jax.ShapeDtypeStruct(arrived.shape, arrived.dtype),
        ),
        in_specs=[flat, one],
        out_specs=(flat, one),
    )(layer, arrived)


def solution(mesh):
    rows = P(("groups", "dev"), None)
    pages = P(("groups", "dev"), None, None)
    placed = (rows, rows, pages, rows, rows, rows, rows, rows, P(), rows, rows)
    placed += (P(None, "dev"), P(None, "dev"), P("dev", None))
    return jax.shard_map(
        on_device, mesh=mesh, in_specs=placed, out_specs=(rows, pages), check_vma=False
    )
```
